32 devices in a mesh: groups: 2 (over x), blocks: 16 (over z, y, core).
Axes of the slice: x: 2, y: 2, z: 4, core: 2. Of those that a mesh axis runs over, the one named last changes fastest.
Arguments:
- features: bfloat16 [163840, 227], P(('groups', 'blocks')), parts along dimension 0, may hold values from -6 to 6
- pair_grid: int32 [16, 96], P('blocks'), may hold values from -4 to 43, as said below
- pair_slot: int32 [16, 96], P('blocks'), may hold values from 0 to 31, as said below
- slot_block: int32 [16, 32], P('blocks'), may hold values from -1 to 63, as said below
- pair_count: int32 [16], P('blocks'), may hold values from 24 to 96, as said below
- coupling: bfloat16 [16, 96, 128, 128], P('blocks'), may hold values from -0.3125 to 0.3125
- mesh_latent: bfloat16 [8192, 512], P('blocks'), may hold values from -6 to 6
- w_in: bfloat16 [227, 512], replicated, may hold values from -0.375 to 0.375
- b_in: float32 [512], replicated, may hold values from -3 to 3
- w_out: bfloat16 [512, 512], replicated, may hold values from -0.25 to 0.25
- b_out: float32 [512], replicated, may hold values from -3 to 3
- grid_gain: float32 [512], replicated, may hold values from 0.1 to 1.9
- w_edge: bfloat16 [512, 512], replicated, may hold values from -0.25 to 0.25
- w_mesh1: bfloat16 [1024, 512], replicated, may hold values from -0.1875 to 0.1875
- b_mesh1: float32 [512], replicated, may hold values from -3 to 3
- w_mesh2: bfloat16 [512, 512], replicated, may hold values from -0.25 to 0.25
- b_mesh2: float32 [512], replicated, may hold values from -3 to 3
- mesh_gain: float32 [512], replicated, may hold values from 0.1 to 1.9
Outputs:
- grid_latent: bfloat16 [163840, 512], P(('groups', 'blocks')), parts along dimension 0
- mesh_out: bfloat16 [16384, 512], P(('groups', 'blocks')), parts along dimension 0
The draws below stay inside these ranges and needn't reach their ends.
There are 2 independent parts, one for each index of `groups`. The reference program is written for one: setup_inputs(seed, part) draws one part's arguments, and reference() takes and returns one part's arrays. A program takes and returns all parts, laid end to end along the dimension named above; an argument that names none is the same for every part. Nothing has to cross between parts.
Inputs may be any that keep to these rules, and one draw needn't show every extreme that they name: `pair_grid`: grid block offsets wrap around the band. `pair_slot`: every entry, live or not, names a slot whose mesh block is not -1. `slot_block`: slot s of a list holds -1 or a mesh block from (s // 2) * 4 to (s // 2 + 1) * 4 - 1; the mesh blocks of one list are distinct; every list has some s // 2 whose 2 slots are all filled. The live entries of a list are its first pair_count ones; some list has all 96.
All inputs are finite; a program needn't handle non-finite values.
Results may differ from the reference program's by a relative error of at most 0.006.
Values may be sent and summed in bfloat16 or wider, within the bound.
A program may use at most 256 MiB of HBM per device.

```python
import jax
import jax.numpy as jnp
from jax import lax

D = 512
FEAT = 227
BS = 128
GB = 40
RIM = 4
PAIRS = 96
CAP = 2
MB_DEV = 4
LISTS = 16
SLOTS = 32
MBLOCKS = 64
MNODES = 8192


def slot_layout(key):
    owner_count = SLOTS // CAP
    live_key, first_key, shift_key = jax.random.split(key, 3)
    live_slots = jax.random.randint(live_key, (LISTS, owner_count, CAP), 0, 2)
    offset_shift = jax.random.randint(shift_key, (), 1, owner_count + 1)
    list_index = jnp.arange(LISTS)[:, None]
    owner_index = jnp.arange(owner_count)[None, :]
    full_owner = owner_index == (list_index + offset_shift) % owner_count
    live_slots = jnp.where(full_owner[:, :, None], 1, live_slots)
    first_local = jax.random.randint(first_key, (LISTS, owner_count), 0, MB_DEV)
    local_block = (first_local[:, :, None] + jnp.arange(CAP)[None, None, :]) % MB_DEV
    mesh_block = owner_index[:, :, None] * MB_DEV + local_block
    mesh_block = jnp.where(live_slots == 1, mesh_block, -1)
    return (live_slots.reshape(LISTS, SLOTS), mesh_block.reshape(LISTS, SLOTS).astype(jnp.int32))


def draw_features(key, part):
    key = jax.random.fold_in(key, 15)
    noise_key, offset_key = jax.random.split(key, 2)
    list_rows = GB * BS
    noise = jax.random.normal(noise_key, (LISTS, list_rows, FEAT), jnp.float32)
    strength = 1.5
    offset = jax.random.normal(offset_key, (LISTS, 1, FEAT), jnp.float32)
    values = jnp.clip(noise + strength * offset, -6.0, 6.0)
    return values.reshape(LISTS * list_rows, FEAT).astype(jnp.bfloat16)


def draw_slot_block(key, part):
    layout = slot_layout(key)
    return layout[1]


def draw_pair_slot(key, part):
    layout = slot_layout(key)
    key = jax.random.fold_in(key, 12)
    live_slots = layout[0]
    live_total = jnp.sum(live_slots, axis=1)
    picks = jax.random.randint(key, (LISTS, PAIRS), 0, live_total[:, None])
    running = jnp.cumsum(live_slots, axis=1)
    chosen = jnp.sum((running[:, None, :] <= picks[:, :, None]).astype(jnp.int32), axis=2)
    return chosen.astype(jnp.int32)


def draw_pair_grid(key, part):
    key = jax.random.fold_in(key, 13)
    return jax.random.randint(key, (LISTS, PAIRS), 0 - RIM, GB + RIM).astype(jnp.int32)


def draw_pair_count(key, part):
    key = jax.random.fold_in(key, 14)
    base_key, dense_key, pick_key = jax.random.split(key, 3)
    counts = jax.random.randint(base_key, (LISTS,), PAIRS // 4, PAIRS // 2 + 1)
    dense_lists = jax.random.randint(dense_key, (LISTS,), 0, 8) == 0
    chosen = jax.random.randint(pick_key, (), 0, LISTS)
    dense_lists = dense_lists | (jnp.arange(LISTS) == chosen)
    return jnp.where(dense_lists, PAIRS, counts).astype(jnp.int32)


def block_scale(key, dims, shards, smallest, largest):
    level, own = 1.0, jax.random.fold_in(key, 6)
    for position, shards_of in shards:
        draws = jnp.exp(jax.random.uniform(jax.random.fold_in(own, position), (shards_of,), jnp.float32, smallest / len(shards), largest / len(shards)))
        level = level * jnp.repeat(draws, dims[position] // shards_of).reshape([-1 if axis == position else 1 for axis in range(len(dims))])
    return level


def scatter_about(own_key, shape, width, most, pieces=(), kind=jnp.bfloat16):
    values = jax.random.normal(own_key, shape, jnp.float32) * width
    if len(pieces) > 0:
        values = block_scale(own_key, shape, pieces, -0.22, 0.18) * values
    return jnp.clip(values, min=-most, max=most).astype(kind)


def setup_inputs(seed: int = 0, part: int = 0) -> dict:
    arg_keys = jax.random.split(jax.random.key(seed), 19)
    own_keys = jax.random.split(jax.random.fold_in(arg_keys[18], part), 19)
    return {
        "features": draw_features(jax.random.fold_in(jax.random.fold_in(arg_keys[18], part), 71), part),
        "pair_grid": draw_pair_grid(jax.random.fold_in(arg_keys[18], 71), part),
        "pair_slot": draw_pair_slot(jax.random.fold_in(arg_keys[18], 71), part),
        "slot_block": draw_slot_block(jax.random.fold_in(arg_keys[18], 71), part),
        "pair_count": draw_pair_count(jax.random.fold_in(arg_keys[18], 71), part),
        "coupling": scatter_about(arg_keys[5], (LISTS, PAIRS, BS, BS), (BS * PAIRS // 32) ** -0.5, 0.3125, ((0, 16),)),
        "mesh_latent": scatter_about(arg_keys[6], (MNODES, D), 1.0, 6.0, ((0, 16),)),
        "w_in": scatter_about(arg_keys[7], (FEAT, D), FEAT ** -0.5, 0.375),
        "b_in": scatter_about(arg_keys[8], (D,), 0.5, 3.0, (), jnp.float32),
        "w_out": scatter_about(arg_keys[9], (D, D), D ** -0.5, 0.25),
        "b_out": scatter_about(arg_keys[10], (D,), 0.5, 3.0, (), jnp.float32),
        "grid_gain": jnp.clip(1.0 + 0.18 * jax.random.normal(arg_keys[11], (D,), jnp.float32), 0.1, 1.9),
        "w_edge": scatter_about(arg_keys[12], (D, D), D ** -0.5, 0.25),
        "w_mesh1": scatter_about(arg_keys[13], (2 * D, D), (2 * D) ** -0.5, 0.1875),
        "b_mesh1": scatter_about(arg_keys[14], (D,), 0.5, 3.0, (), jnp.float32),
        "w_mesh2": scatter_about(arg_keys[15], (D, D), D ** -0.5, 0.25),
        "b_mesh2": scatter_about(arg_keys[16], (D,), 0.5, 3.0, (), jnp.float32),
        "mesh_gain": jnp.clip(1.0 + 0.18 * jax.random.normal(arg_keys[17], (D,), jnp.float32), 0.1, 1.9),
    }


norm_eps = 1e-05

def layer_norm(values, gain):
    centred = values - lax.optimization_barrier(jnp.mean(values, axis=-1, keepdims=True))
    spread = lax.optimization_barrier(jnp.mean(centred * centred, axis=-1, keepdims=True))
    return centred * lax.rsqrt(spread + norm_eps) * gain

def reference(features, pair_grid, pair_slot, slot_block, pair_count, coupling, mesh_latent, w_in, b_in, w_out, b_out, grid_gain, w_edge, w_mesh1, b_mesh1, w_mesh2, b_mesh2, mesh_gain):
    activation = jax.nn.silu(jnp.dot(features, w_in, preferred_element_type=jnp.float32) + b_in).astype(jnp.bfloat16)
    grid_latent = layer_norm(jnp.dot(activation, w_out, preferred_element_type=jnp.float32) + b_out, grid_gain).astype(jnp.bfloat16)
    edge_rows = jnp.dot(grid_latent, w_edge, preferred_element_type=jnp.float32).astype(jnp.bfloat16)
    block_total = LISTS * GB
    edge_blocks = edge_rows.reshape(block_total, BS, D)
    pair_index = jnp.arange(PAIRS, dtype=jnp.int32)

    def one_list(totals, inputs):
        list_index, grid_offsets, slots_of_pairs, blocks_of_slots, live_count, couplings = inputs
        where_from = ((list_index * GB + grid_offsets) % block_total).astype(jnp.int32)
        sources = edge_blocks[where_from].astype(jnp.float32)
        message = jnp.einsum('pqr,prf->pqf', couplings.astype(jnp.float32), sources, precision=lax.Precision.HIGHEST)
        target = blocks_of_slots[slots_of_pairs]
        target = jnp.where(pair_index < live_count, target, MBLOCKS)
        return (totals.at[target].add(message, mode='drop'), None)
    start_totals = jnp.zeros((MBLOCKS, BS, D), jnp.float32)
    aggregate, unused = lax.scan(one_list, start_totals, (jnp.arange(LISTS, dtype=jnp.int32), pair_grid, pair_slot, slot_block, pair_count, coupling))
    aggregate_half = aggregate.reshape(MNODES, D).astype(jnp.bfloat16)
    mesh_hidden = jax.nn.silu(jnp.dot(mesh_latent, w_mesh1[:D], preferred_element_type=jnp.float32) + jnp.dot(aggregate_half, w_mesh1[D:], preferred_element_type=jnp.float32) + b_mesh1).astype(jnp.bfloat16)
    update = layer_norm(jnp.dot(mesh_hidden, w_mesh2, preferred_element_type=jnp.float32) + b_mesh2, mesh_gain)
    mesh_out = (mesh_latent.astype(jnp.float32) + update).astype(jnp.bfloat16)
    return (grid_latent, mesh_out)
```

```python
import functools

import jax
import jax.numpy as jnp
from jax import lax
from jax.experimental import pallas as pl
from jax.experimental.pallas import tpu as pltpu
from jax.sharding import PartitionSpec as P

RIM = 4

norm_eps = 1e-05
vmem_bytes = 56 * 1024 * 1024


def silu(values):
    return 0.5 * values * (1.0 + jnp.tanh(0.5 * values))


def layer_norm(values, gain):
    centred = values - jnp.mean(values, axis=-1, keepdims=True)
    spread = jnp.mean(centred * centred, axis=-1, keepdims=True)
    return centred * lax.rsqrt(spread + norm_eps) * gain


def grid_rows(features, w_in, b_in, w_out, b_out, grid_gain, w_edge):
    hidden = jnp.dot(features[...], w_in[...], preferred_element_type=jnp.float32) + b_in[...]
    activation = silu(hidden).astype(jnp.bfloat16)
    latent = jnp.dot(activation, w_out[...], preferred_element_type=jnp.float32) + b_out[...]
    latent = layer_norm(latent, grid_gain[...]).astype(jnp.bfloat16)
    edges = jnp.dot(latent, w_edge[...], preferred_element_type=jnp.float32).astype(jnp.bfloat16)
    return latent, edges


def rim_kernel(features, w_in, b_in, w_out, b_out, grid_gain, w_edge, latent_out, head, tail):
    latent, edges = grid_rows(features, w_in, b_in, w_out, b_out, grid_gain, w_edge)
    latent_out[...] = latent

    @pl.when(pl.program_id(0) == 0)
    def _():
        head[...] = edges

    @pl.when(pl.program_id(0) == 1)
    def _():
        tail[...] = edges


def inner_kernel(
    features, w_in, b_in, w_out, b_out, grid_gain, w_edge, rim_latent, latent_out, edges_out
):
    latent, edges = grid_rows(features, w_in, b_in, w_out, b_out, grid_gain, w_edge)
    latent_out[...] = latent
    edges_out[...] = edges


def pair_kernel(
    pair_grid,
    pair_slot,
    slot_block,
    pair_count,
    left,
    head,
    inner,
    tail,
    right,
    coupling,
    sums_out,
    edges,
    weights,
    acc,
    stage,
    load_sem,
    store_sem,
):
    pairs = weights.shape[0]
    blocks = stage.shape[0]
    inner_blocks = inner.shape[0]
    begin = 0
    loads = []
    for position, part in enumerate((left, head, inner, tail, right)):
        count = part.shape[0]
        loads.append(
            pltpu.make_async_copy(part, edges.at[pl.ds(begin, count)], load_sem.at[position])
        )
        begin += count
    loads.append(pltpu.make_async_copy(coupling.at[0], weights, load_sem.at[5]))
    for load in loads:
        load.start()

    @pl.loop(0, blocks)
    def _(block):
        acc[block] = jnp.zeros(acc.shape[1:], jnp.float32)

    for load in loads:
        load.wait()
    live = pair_count[0]
    unroll = 4

    @pl.loop(0, (live + unroll - 1) // unroll)
    def _(group):
        for lane in range(unroll):
            pair = group * unroll + lane
            target = slot_block[0, pair_slot[0, pair]]
            target = jnp.where(pair < live, target, blocks)
            acc[target] += jnp.dot(
                weights[pair],
                edges[pair_grid[0, pair] + RIM],
                preferred_element_type=jnp.float32,
            )

    piece = store_sem.shape[0]
    step = blocks // piece

    def store(index):
        span = pl.ds(index * step, step)
        return pltpu.make_async_copy(stage.at[span], sums_out.at[span], store_sem.at[index])

    @pl.loop(0, piece)
    def _(index):
        for offset in range(step):
            block = index * step + offset
            stage[block] = acc[block].astype(jnp.bfloat16)
        store(index).start()

    @pl.loop(0, piece)
    def _(index):
        store(index).wait()


def ring_kernel(
    device_total,
    sums,
    mesh_latent,
    w_mesh1,
    b_mesh1,
    w_mesh2,
    b_mesh2,
    mesh_gain,
    mesh_out,
    own,
    peer,
    got,
    hidden,
    own_sem,
    peer_send,
    peer_recv,
    ring_send,
    ring_recv,
):
    chips = device_total // 2
    per_owner = own.shape[1]
    half = per_owner // 2
    block_size = own.shape[2]
    width = own.shape[3]
    me = lax.axis_index("blocks")
    chip = me // 2
    core = me % 2

    def chip_at(place):
        return jnp.where(place < chips // 2, 2 * place, 2 * (chips - 1 - place) + 1)

    place = jnp.where(chip % 2 == 0, chip // 2, chips - 1 - chip // 2)
    after = 2 * chip_at((place + 1) % chips) + core
    before = 2 * chip_at((place + chips - 1) % chips) + core
    other = 2 * chip + 1 - core

    barrier = pltpu.get_barrier_semaphore()
    for device in (other, after, before):
        pl.semaphore_signal(
            barrier, inc=1, device_id={"blocks": device}, device_id_type=pl.DeviceIdType.MESH
        )

    def owner_chip(step, way):
        if way == 0:
            return chip_at((place + 2 * chips - 1 - step) % chips)
        return chip_at((place + 1 + step) % chips)

    def own_copy(step, way):
        first = (2 * owner_chip(step, way) + core) * per_owner + way * half
        return pltpu.make_async_copy(
            sums.at[pl.ds(first, half)],
            own.at[step, pl.ds(way * half, half)],
            own_sem.at[step, way],
        )

    def peer_copy(step, way):
        first = (2 * owner_chip(step, way) + 1 - core) * per_owner + way * half
        return pltpu.make_async_remote_copy(
            src_ref=sums.at[pl.ds(first, half)],
            dst_ref=peer.at[step, pl.ds(way * half, half)],
            send_sem=peer_send.at[step, way],
            recv_sem=peer_recv.at[step, way],
            device_id={"blocks": other},
            device_id_type=pl.DeviceIdType.MESH,
        )

    def ring_copy(step, chain):
        return pltpu.make_async_remote_copy(
            src_ref=own.at[step, chain],
            dst_ref=got.at[step, chain],
            send_sem=ring_send.at[step, chain],
            recv_sem=ring_recv.at[step, chain],
            device_id={"blocks": after if chain < half else before},
            device_id_type=pl.DeviceIdType.MESH,
        )

    ahead = 3

    @pl.loop(0, chips)
    def _(step):
        for way in range(2):
            own_copy(step, way).start()

    pl.semaphore_wait(barrier, 3)
    for step in range(ahead):
        for way in range(2):
            peer_copy(step, way).start()

    def both(step, chain):
        return own[step, chain].astype(jnp.float32) + peer[step, chain].astype(jnp.float32)

    def arrive(step):
        for way in range(2):
            own_copy(step, way).wait()
            peer_copy(step, way).wait_recv()

    order = [chain for pair in zip(range(half), range(half, per_owner)) for chain in pair]
    arrive(0)
    for chain in order:
        own[0, chain] = both(0, chain).astype(jnp.bfloat16)
        ring_copy(0, chain).start()

    hidden[...] = (
        jnp.dot(mesh_latent[...], w_mesh1[:width], preferred_element_type=jnp.float32)
        + b_mesh1[...]
    )

    @pl.loop(1, chips - 1)
    def _(step):
        @pl.when(step + ahead - 1 < chips)
        def _():
            for way in range(2):
                peer_copy(step + ahead - 1, way).start()

        arrive(step)
        for chain in order:
            ring_copy(step - 1, chain).wait_recv()
            total = both(step, chain) + got[step - 1, chain].astype(jnp.float32)
            own[step, chain] = total.astype(jnp.bfloat16)
            ring_copy(step, chain).start()

    last = chips - 1
    arrive(last)
    for chain in order:
        ring_copy(last - 1, chain).wait_recv()
        total = both(last, chain) + got[last - 1, chain].astype(jnp.float32)
        rows = pl.ds(chain * block_size, block_size)
        value = hidden[rows] + jnp.dot(
            total.astype(jnp.bfloat16), w_mesh1[width:], preferred_element_type=jnp.float32
        )
        value = silu(value).astype(jnp.bfloat16)
        value = jnp.dot(value, w_mesh2[...], preferred_element_type=jnp.float32) + b_mesh2[...]
        update = layer_norm(value, mesh_gain[...])
        mesh_out[rows] = (mesh_latent[rows].astype(jnp.float32) + update).astype(jnp.bfloat16)

    @pl.loop(0, chips)
    def _(step):
        for way in range(2):
            peer_copy(step, way).wait_send()

    @pl.loop(0, chips - 1)
    def _(step):
        for chain in range(per_owner):
            ring_copy(step, chain).wait_send()


def on_device(
    features,
    pair_grid,
    pair_slot,
    slot_block,
    pair_count,
    coupling,
    mesh_latent,
    w_in,
    b_in,
    w_out,
    b_out,
    grid_gain,
    w_edge,
    w_mesh1,
    b_mesh1,
    w_mesh2,
    b_mesh2,
    mesh_gain,
):
    block_size = coupling.shape[-1]
    pair_total = coupling.shape[1]
    width = w_edge.shape[1]
    rows, feature_width = features.shape
    tile = RIM * block_size
    tiles = rows // tile
    owner_total = lax.axis_size("blocks")
    own_blocks = mesh_latent.shape[0] // block_size
    mesh_blocks = own_blocks * owner_total
    bf16 = jnp.bfloat16
    f32 = jnp.float32

    def flat(vector):
        return vector.reshape(1, -1)

    params = (w_in, flat(b_in), w_out, flat(b_out), flat(grid_gain), w_edge)
    param_specs = [pl.BlockSpec(param.shape, lambda i: (0, 0)) for param in params]

    def cost(steps):
        work = 2 * tile * width * (feature_width + 2 * width)
        return pl.CostEstimate(
            flops=steps * work,
            bytes_accessed=steps * tile * (feature_width + 2 * width) * 2,
            transcendentals=steps * tile * width,
        )

    whole_tile = pl.BlockSpec((tile, width), lambda i: (0, 0))
    rim_latent, head, tail = pl.pallas_call(
        rim_kernel,
        grid=(2,),
        in_specs=[pl.BlockSpec((tile, feature_width), lambda i: (i * (tiles - 1), 0))]
        + param_specs,
        out_specs=[
            pl.BlockSpec((tile, width), lambda i: (i * (tiles - 1), 0)),
            whole_tile,
            whole_tile,
        ],
        out_shape=[
            jax.ShapeDtypeStruct((rows, width), bf16),
            jax.ShapeDtypeStruct((tile, width), bf16),
            jax.ShapeDtypeStruct((tile, width), bf16),
        ],
        cost_estimate=cost(2),
        compiler_params=pltpu.CompilerParams(vmem_limit_bytes=vmem_bytes),
        name="rim_rows",
    )(features, *params)

    left = lax.ppermute(tail, "blocks", [(i, (i + 1) % owner_total) for i in range(owner_total)])
    right = lax.ppermute(head, "blocks", [((i + 1) % owner_total, i) for i in range(owner_total)])

    grid_latent, inner = pl.pallas_call(
        inner_kernel,
        grid=(tiles - 2,),
        in_specs=[pl.BlockSpec((tile, feature_width), lambda i: (i + 1, 0))]
        + param_specs
        + [pl.BlockSpec(memory_space=pl.ANY)],
        out_specs=[
            pl.BlockSpec((tile, width), lambda i: (i + 1, 0)),
            pl.BlockSpec((tile, width), lambda i: (i, 0)),
        ],
        out_shape=[
            jax.ShapeDtypeStruct((rows, width), bf16),
            jax.ShapeDtypeStruct((rows - 2 * tile, width), bf16),
        ],
        input_output_aliases={7: 0},
        cost_estimate=cost(tiles - 2),
        compiler_params=pltpu.CompilerParams(vmem_limit_bytes=vmem_bytes),
        name="inner_rows",
    )(features, *params, rim_latent)

    edge_parts = [
        part.reshape(-1, block_size, width) for part in (left, head, inner, tail, right)
    ]
    edge_total = sum(part.shape[0] for part in edge_parts)
    smem = pl.BlockSpec(memory_space=pltpu.SMEM)
    anywhere = pl.BlockSpec(memory_space=pl.ANY)
    sums = pl.pallas_call(
        pair_kernel,
        in_specs=[smem] * 4 + [anywhere] * 6,
        out_specs=anywhere,
        out_shape=jax.ShapeDtypeStruct((mesh_blocks, block_size, width), bf16),
        scratch_shapes=[
            pltpu.VMEM((edge_total, block_size, width), bf16),
            pltpu.VMEM((pair_total, block_size, block_size), bf16),
            pltpu.VMEM((mesh_blocks + 1, block_size, width), f32),
            pltpu.VMEM((mesh_blocks, block_size, width), bf16),
            pltpu.SemaphoreType.DMA((6,)),
            pltpu.SemaphoreType.DMA((owner_total,)),
        ],
        compiler_params=pltpu.CompilerParams(vmem_limit_bytes=62 * 1024 * 1024),
        name="pair_sums",
    )(pair_grid, pair_slot, slot_block, pair_count, *edge_parts, coupling)

    chips = owner_total // 2
    vmem = pl.BlockSpec(memory_space=pltpu.VMEM)
    mesh_out = pl.pallas_call(
        functools.partial(ring_kernel, owner_total),
        in_specs=[anywhere] + [vmem] * 6,
        out_specs=vmem,
        out_shape=jax.ShapeDtypeStruct(mesh_latent.shape, bf16),
        scratch_shapes=[
            pltpu.VMEM((chips, own_blocks, block_size, width), bf16),
            pltpu.VMEM((chips, own_blocks, block_size, width), bf16),
            pltpu.VMEM((chips - 1, own_blocks, block_size, width), bf16),
            pltpu.VMEM(mesh_latent.shape, f32),
            pltpu.SemaphoreType.DMA((chips, 2)),
            pltpu.SemaphoreType.DMA((chips, 2)),
            pltpu.SemaphoreType.DMA((chips, 2)),
            pltpu.SemaphoreType.DMA((chips - 1, own_blocks)),
            pltpu.SemaphoreType.DMA((chips - 1, own_blocks)),
        ],
        compiler_params=pltpu.CompilerParams(
            collective_id=0, has_side_effects=True, vmem_limit_bytes=vmem_bytes
        ),
        name="ring_sums",
    )(sums, mesh_latent, w_mesh1, flat(b_mesh1), w_mesh2, flat(b_mesh2), flat(mesh_gain))
    return (grid_latent, mesh_out)


def solution(mesh):
    in_specs = (
        P(("groups", "blocks"), None),
        P("blocks", None),
        P("blocks", None),
        P("blocks", None),
        P("blocks"),
        P("blocks", None, None, None),
        P("blocks", None),
        P(),
        P(),
        P(),
        P(),
        P(),
        P(),
        P(),
        P(),
        P(),
        P(),
        P(),
    )
    out_specs = (P(("groups", "blocks"), None), P(("groups", "blocks"), None))
    return jax.shard_map(
        on_device, mesh=mesh, in_specs=in_specs, out_specs=out_specs, check_vma=False
    )
```

```python
import functools

import jax
import jax.numpy as jnp
from jax import lax
from jax.experimental import pallas as pl
from jax.experimental.pallas import tpu as pltpu
from jax.sharding import PartitionSpec as P

RIM = 4
cap = 2

norm_eps = 1e-05
vmem_bytes = 56 * 1024 * 1024
chain_rows = 128
unroll = 8


def silu(values):
    return 0.5 * values * (1.0 + jnp.tanh(0.5 * values))


def layer_norm(values, gain):
    centred = values - jnp.mean(values, axis=-1, keepdims=True)
    spread = jnp.mean(centred * centred, axis=-1, keepdims=True)
    return centred * lax.rsqrt(spread + norm_eps) * gain


def grid_rows(features, w_in, b_in, w_out, b_out, grid_gain, w_edge):
    hidden = lax.dot_general(
        features, w_in[...], (((0,), (0,)), ((), ())), preferred_element_type=jnp.float32
    )
    activation = silu(hidden + b_in[...]).astype(jnp.bfloat16)
    latent = jnp.dot(activation, w_out[...], preferred_element_type=jnp.float32) + b_out[...]
    latent = layer_norm(latent, grid_gain[...]).astype(jnp.bfloat16)
    edges = jnp.dot(latent, w_edge[...], preferred_element_type=jnp.float32).astype(jnp.bfloat16)
    return latent, edges


def grid_kernel(
    features, w_in, b_in, w_out, b_out, grid_gain, w_edge, latent_out, edges_out
):
    latent, edges = grid_rows(features[...], w_in, b_in, w_out, b_out, grid_gain, w_edge)
    latent_out[...] = latent
    edges_out[...] = edges


def pair_kernel(
    pair_grid,
    pair_slot,
    slot_block,
    pair_count,
    features,
    w_in,
    b_in,
    w_out,
    b_out,
    grid_gain,
    w_edge,
    left,
    right,
    done,
    coupling,
    latent_in,
    latent_out,
    sums_out,
    edges,
    weights,
    acc,
    stage,
    zeros,
    held,
    load_sem,
    store_sem,
    latent_sem,
):
    slots = stage.shape[0]
    block_size, width = zeros.shape
    blocks = sums_out.shape[0]
    owners = slots // cap
    per_owner = blocks // owners
    rest = held.shape[0]
    rim = left.shape[1]
    done_rows = done.shape[0]
    loads = [
        pltpu.make_async_copy(coupling.at[0], weights, load_sem.at[0]),
        pltpu.make_async_copy(done, edges.at[pl.ds(rim, done_rows)], load_sem.at[1]),
    ]
    for load in loads:
        load.start()

    zeros[...] = jnp.zeros(zeros.shape, jnp.bfloat16)

    @pl.loop(0, owners)
    def _(owner):
        for offset in range(per_owner):
            block = owner * per_owner + offset
            used = slot_block[0, owner * cap] == block
            for extra in range(1, cap):
                used = used | (slot_block[0, owner * cap + extra] == block)

            @pl.when(jnp.logical_not(used))
            def _():
                pltpu.make_async_copy(zeros, sums_out.at[block], store_sem.at[block]).start()

    @pl.loop(0, slots)
    def _(slot):
        acc[slot] = jnp.zeros(acc.shape[1:], jnp.float32)

    params = (w_in, b_in, w_out, b_out, grid_gain, w_edge)
    latent, rest_edges = grid_rows(features[...], *params)
    held[...] = latent
    latent_copy = pltpu.make_async_copy(
        held, latent_out.at[pl.ds(done_rows, rest)], latent_sem
    )
    latent_copy.start()
    edges[pl.ds(rim + done_rows, rest)] = rest_edges
    unused, rim_edges = grid_rows(
        jnp.concatenate([left[...], right[...]], axis=1), *params
    )
    edges[pl.ds(0, rim)] = rim_edges[:rim]
    edges[pl.ds(rim + done_rows + rest, rim)] = rim_edges[rim:]

    for load in loads:
        load.wait()
    live = pair_count[0]

    @pl.loop(0, (live + unroll - 1) // unroll)
    def _(group):
        for lane in range(unroll):
            pair = group * unroll + lane
            target = jnp.where(pair < live, pair_slot[0, pair], slots)
            first = pl.multiple_of((pair_grid[0, pair] + RIM) * block_size, block_size)
            acc[target] += jnp.dot(
                weights[pair],
                edges[pl.ds(first, block_size)],
                preferred_element_type=jnp.float32,
            )

    @pl.loop(0, slots)
    def _(slot):
        stage[slot] = acc[slot].astype(jnp.bfloat16)
        block = slot_block[0, slot]

        @pl.when(block >= 0)
        def _():
            pltpu.make_async_copy(
                stage.at[slot], sums_out.at[block], store_sem.at[block]
            ).start()

    latent_copy.wait()

    @pl.loop(0, blocks)
    def _(block):
        pltpu.make_async_copy(zeros, sums_out.at[block], store_sem.at[block]).wait()


def ring_kernel(
    device_total,
    sums,
    mesh_latent,
    w_mesh1,
    b_mesh1,
    w_mesh2,
    b_mesh2,
    mesh_gain,
    mesh_out,
    own,
    peer,
    got,
    hidden,
    own_sem,
    peer_send,
    peer_recv,
    ring_send,
    ring_recv,
):
    chips = device_total // 2
    per_owner = own.shape[1]
    half = per_owner // 2
    width = own.shape[2]
    chains = per_owner // chain_rows
    me = lax.axis_index("blocks")
    chip = me // 2
    core = me % 2

    def chip_at(place):
        return jnp.where(place < chips // 2, 2 * place, 2 * (chips - 1 - place) + 1)

    place = jnp.where(chip % 2 == 0, chip // 2, chips - 1 - chip // 2)
    after = 2 * chip_at((place + 1) % chips) + core
    before = 2 * chip_at((place + chips - 1) % chips) + core
    other = 2 * chip + 1 - core

    barrier = pltpu.get_barrier_semaphore()
    for device in (other, after, before):
        pl.semaphore_signal(
            barrier, inc=1, device_id={"blocks": device}, device_id_type=pl.DeviceIdType.MESH
        )

    def owner_chip(step, way):
        if way == 0:
            return chip_at((place + 2 * chips - 1 - step) % chips)
        return chip_at((place + 1 + step) % chips)

    def own_copy(step, way):
        first = (2 * owner_chip(step, way) + core) * per_owner + way * half
        return pltpu.make_async_copy(
            sums.at[pl.ds(first, half)],
            own.at[step, pl.ds(way * half, half)],
            own_sem.at[step, way],
        )

    def peer_copy(step, way):
        first = (2 * owner_chip(step, way) + 1 - core) * per_owner + way * half
        return pltpu.make_async_remote_copy(
            src_ref=sums.at[pl.ds(first, half)],
            dst_ref=peer.at[step, pl.ds(way * half, half)],
            send_sem=peer_send.at[step, way],
            recv_sem=peer_recv.at[step, way],
            device_id={"blocks": other},
            device_id_type=pl.DeviceIdType.MESH,
        )

    def rows_of(chain):
        return pl.ds(chain * chain_rows, chain_rows)

    def ring_copy(step, chain):
        return pltpu.make_async_remote_copy(
            src_ref=own.at[step, rows_of(chain)],
            dst_ref=got.at[step, rows_of(chain)],
            send_sem=ring_send.at[step, chain],
            recv_sem=ring_recv.at[step, chain],
            device_id={"blocks": after if chain < chains // 2 else before},
            device_id_type=pl.DeviceIdType.MESH,
        )

    ahead = 3

    @pl.loop(0, chips)
    def _(step):
        for way in range(2):
            own_copy(step, way).start()

    pl.semaphore_wait(barrier, 3)
    for step in range(ahead):
        for way in range(2):
            peer_copy(step, way).start()

    def both(step, chain):
        rows = rows_of(chain)
        return own[step, rows].astype(jnp.float32) + peer[step, rows].astype(jnp.float32)

    def arrive(step):
        for way in range(2):
            own_copy(step, way).wait()
            peer_copy(step, way).wait_recv()

    order = [
        chain for pair in zip(range(chains // 2), range(chains // 2, chains)) for chain in pair
    ]
    arrive(0)
    for chain in order:
        own[0, rows_of(chain)] = both(0, chain).astype(jnp.bfloat16)
        ring_copy(0, chain).start()

    hidden[...] = (
        jnp.dot(mesh_latent[...], w_mesh1[:width], preferred_element_type=jnp.float32)
        + b_mesh1[...]
    )

    @pl.loop(1, chips - 1)
    def _(step):
        @pl.when(step + ahead - 1 < chips)
        def _():
            for way in range(2):
                peer_copy(step + ahead - 1, way).start()

        arrive(step)
        for chain in order:
            ring_copy(step - 1, chain).wait_recv()
            total = both(step, chain) + got[step - 1, rows_of(chain)].astype(jnp.float32)
            own[step, rows_of(chain)] = total.astype(jnp.bfloat16)
            ring_copy(step, chain).start()

    last = chips - 1
    arrive(last)
    for chain in order:
        ring_copy(last - 1, chain).wait_recv()
        total = both(last, chain) + got[last - 1, rows_of(chain)].astype(jnp.float32)
        rows = rows_of(chain)
        value = hidden[rows] + jnp.dot(
            total.astype(jnp.bfloat16), w_mesh1[width:], preferred_element_type=jnp.float32
        )
        value = silu(value).astype(jnp.bfloat16)
        value = jnp.dot(value, w_mesh2[...], preferred_element_type=jnp.float32) + b_mesh2[...]
        update = layer_norm(value, mesh_gain[...])
        mesh_out[rows] = (mesh_latent[rows].astype(jnp.float32) + update).astype(jnp.bfloat16)

    @pl.loop(0, chips)
    def _(step):
        for way in range(2):
            peer_copy(step, way).wait_send()

    @pl.loop(0, chips - 1)
    def _(step):
        for chain in range(chains):
            ring_copy(step, chain).wait_send()


def on_device(
    features,
    pair_grid,
    pair_slot,
    slot_block,
    pair_count,
    coupling,
    mesh_latent,
    w_in,
    b_in,
    w_out,
    b_out,
    grid_gain,
    w_edge,
    w_mesh1,
    b_mesh1,
    w_mesh2,
    b_mesh2,
    mesh_gain,
):
    block_size = coupling.shape[-1]
    pair_total = coupling.shape[1]
    width = w_edge.shape[1]
    rows, feature_width = features.shape
    tile = RIM * block_size
    tiles = rows // tile
    owner_total = lax.axis_size("blocks")
    slot_total = slot_block.shape[1]
    features = features.T
    own_blocks = mesh_latent.shape[0] // block_size
    mesh_blocks = own_blocks * owner_total
    bf16 = jnp.bfloat16
    f32 = jnp.float32

    def flat(vector):
        return vector.reshape(1, -1)

    params = (w_in, flat(b_in), w_out, flat(b_out), flat(grid_gain), w_edge)
    param_specs = [pl.BlockSpec(param.shape, lambda i: (0, 0)) for param in params]
    wide = 2 * tile
    done_steps = rows // wide - 1
    smem = pl.BlockSpec(memory_space=pltpu.SMEM)
    anywhere = pl.BlockSpec(memory_space=pl.ANY)
    vmem = pl.BlockSpec(memory_space=pltpu.VMEM)
    semaphore = pltpu.SemaphoreType.DMA
    count = done_steps * wide

    left = lax.ppermute(
        features[:, rows - tile :],
        "blocks",
        [(i, (i + 1) % owner_total) for i in range(owner_total)],
    )
    right = lax.ppermute(
        features[:, :tile], "blocks", [((i + 1) % owner_total, i) for i in range(owner_total)]
    )

    latent, done = pl.pallas_call(
        grid_kernel,
        grid=(done_steps,),
        in_specs=[pl.BlockSpec((feature_width, wide), lambda i: (0, i))] + param_specs,
        out_specs=[
            pl.BlockSpec((wide, width), lambda i: (i, 0)),
            pl.BlockSpec((wide, width), lambda i: (i, 0)),
        ],
        out_shape=[
            jax.ShapeDtypeStruct((rows, width), bf16),
            jax.ShapeDtypeStruct((count, width), bf16),
        ],
        cost_estimate=pl.CostEstimate(
            flops=count * 2 * width * (feature_width + 2 * width),
            bytes_accessed=count * (feature_width + 2 * width) * 2,
            transcendentals=count * width,
        ),
        compiler_params=pltpu.CompilerParams(vmem_limit_bytes=vmem_bytes),
        name="grid_rows",
    )(features, *params)

    grid_latent, sums = pl.pallas_call(
        pair_kernel,
        grid=(1,),
        in_specs=[smem] * 4
        + [pl.BlockSpec((feature_width, wide), lambda i: (0, done_steps))]
        + param_specs
        + [vmem, vmem, anywhere, anywhere, anywhere],
        out_specs=[anywhere, anywhere],
        out_shape=[
            jax.ShapeDtypeStruct((rows, width), bf16),
            jax.ShapeDtypeStruct((mesh_blocks, block_size, width), bf16),
        ],
        scratch_shapes=[
            pltpu.VMEM((rows + 2 * tile, width), bf16),
            pltpu.VMEM((pair_total, block_size, block_size), bf16),
            pltpu.VMEM((slot_total + 1, block_size, width), f32),
            pltpu.VMEM((slot_total, block_size, width), bf16),
            pltpu.VMEM((block_size, width), bf16),
            pltpu.VMEM((wide, width), bf16),
            semaphore((2,)),
            semaphore((mesh_blocks,)),
            semaphore,
        ],
        input_output_aliases={15: 0},
        compiler_params=pltpu.CompilerParams(vmem_limit_bytes=vmem_bytes),
        name="pair_sums",
    )(
        pair_grid,
        pair_slot,
        slot_block,
        pair_count,
        features,
        *params,
        left,
        right,
        done,
        coupling,
        latent,
    )

    chips = owner_total // 2
    mesh_rows = own_blocks * block_size
    mesh_out = pl.pallas_call(
        functools.partial(ring_kernel, owner_total),
        in_specs=[anywhere] + [vmem] * 6,
        out_specs=vmem,
        out_shape=jax.ShapeDtypeStruct(mesh_latent.shape, bf16),
        scratch_shapes=[
            pltpu.VMEM((chips, mesh_rows, width), bf16),
            pltpu.VMEM((chips, mesh_rows, width), bf16),
            pltpu.VMEM((chips - 1, mesh_rows, width), bf16),
            pltpu.VMEM(mesh_latent.shape, f32),
            pltpu.SemaphoreType.DMA((chips, 2)),
            pltpu.SemaphoreType.DMA((chips, 2)),
            pltpu.SemaphoreType.DMA((chips, 2)),
            pltpu.SemaphoreType.DMA((chips - 1, mesh_rows // chain_rows)),
            pltpu.SemaphoreType.DMA((chips - 1, mesh_rows // chain_rows)),
        ],
        compiler_params=pltpu.CompilerParams(
            collective_id=0, has_side_effects=True, vmem_limit_bytes=vmem_bytes
        ),
        name="ring_sums",
    )(sums.reshape(-1, width), mesh_latent, w_mesh1, flat(b_mesh1), w_mesh2, flat(b_mesh2), flat(mesh_gain))
    return (grid_latent, mesh_out)


def solution(mesh):
    in_specs = (
        P(("groups", "blocks"), None),
        P("blocks", None),
        P("blocks", None),
        P("blocks", None),
        P("blocks"),
        P("blocks", None, None, None),
        P("blocks", None),
        P(),
        P(),
        P(),
        P(),
        P(),
        P(),
        P(),
        P(),
        P(),
        P(),
        P(),
    )
    out_specs = (P(("groups", "blocks"), None), P(("groups", "blocks"), None))
    return jax.shard_map(
        on_device, mesh=mesh, in_specs=in_specs, out_specs=out_specs, check_vma=False
    )
```

```python
import functools

import jax
import jax.numpy as jnp
from jax import lax
from jax.experimental import pallas as pl
from jax.experimental.pallas import tpu as pltpu
from jax.sharding import PartitionSpec as P

RIM = 4
cap = 2

norm_eps = 1e-05
mib = 1024 * 1024
grid_mib = 56
spare_mib = 60
chain_rows = 128
unroll = 16


def silu(values):
    return 0.5 * values * (1.0 + jnp.tanh(0.5 * values))


def layer_norm(values, gain):
    centred = values - jnp.mean(values, axis=-1, keepdims=True)
    spread = jnp.mean(centred * centred, axis=-1, keepdims=True)
    return centred * lax.rsqrt(spread + norm_eps) * gain


def grid_rows(features, w_in, b_in, w_out, b_out, grid_gain, w_edge):
    hidden = lax.dot_general(
        features, w_in[...], (((0,), (0,)), ((), ())), preferred_element_type=jnp.float32
    )
    activation = silu(hidden + b_in[...]).astype(jnp.bfloat16)
    latent = jnp.dot(activation, w_out[...], preferred_element_type=jnp.float32) + b_out[...]
    latent = layer_norm(latent, grid_gain[...]).astype(jnp.bfloat16)
    edges = jnp.dot(latent, w_edge[...], preferred_element_type=jnp.float32).astype(jnp.bfloat16)
    return latent, edges


def grid_kernel(
    features, w_in, b_in, w_out, b_out, grid_gain, w_edge, latent_out, edges_out
):
    latent, edges = grid_rows(features[...], w_in, b_in, w_out, b_out, grid_gain, w_edge)
    latent_out[...] = latent
    edges_out[...] = edges


def pair_kernel(
    pair_grid,
    pair_slot,
    slot_block,
    pair_count,
    features,
    w_in,
    b_in,
    w_out,
    b_out,
    grid_gain,
    w_edge,
    left,
    right,
    done,
    coupling,
    latent_in,
    latent_out,
    sums_out,
    edges,
    weights,
    acc,
    stage,
    zeros,
    held,
    load_sem,
    store_sem,
    latent_sem,
):
    slots = stage.shape[0]
    block_size, width = zeros.shape
    blocks = sums_out.shape[0]
    owners = slots // cap
    per_owner = blocks // owners
    rest = held.shape[0]
    rim = left.shape[1]
    done_rows = done.shape[0]
    loads = [
        pltpu.make_async_copy(coupling.at[0], weights, load_sem.at[0]),
        pltpu.make_async_copy(done, edges.at[pl.ds(rim, done_rows)], load_sem.at[1]),
    ]
    for load in loads:
        load.start()

    zeros[...] = jnp.zeros(zeros.shape, jnp.bfloat16)

    @pl.loop(0, owners)
    def _(owner):
        for offset in range(per_owner):
            block = owner * per_owner + offset
            used = slot_block[0, owner * cap] == block
            for extra in range(1, cap):
                used = used | (slot_block[0, owner * cap + extra] == block)

            @pl.when(jnp.logical_not(used))
            def _():
                pltpu.make_async_copy(zeros, sums_out.at[block], store_sem.at[block]).start()

    @pl.loop(0, slots)
    def _(slot):
        acc[slot] = jnp.zeros(acc.shape[1:], jnp.float32)

    params = (w_in, b_in, w_out, b_out, grid_gain, w_edge)
    latent, rest_edges = grid_rows(features[...], *params)
    held[...] = latent
    latent_copy = pltpu.make_async_copy(
        held, latent_out.at[pl.ds(done_rows, rest)], latent_sem
    )
    latent_copy.start()
    edges[pl.ds(rim + done_rows, rest)] = rest_edges
    unused, rim_edges = grid_rows(
        jnp.concatenate([left[...], right[...]], axis=1), *params
    )
    edges[pl.ds(0, rim)] = rim_edges[:rim]
    edges[pl.ds(rim + done_rows + rest, rim)] = rim_edges[rim:]

    for load in loads:
        load.wait()
    live = pair_count[0]

    @pl.loop(0, (live + unroll - 1) // unroll)
    def _(group):
        for lane in range(unroll):
            pair = group * unroll + lane
            target = jnp.where(pair < live, pair_slot[0, pair], slots)
            first = pl.multiple_of((pair_grid[0, pair] + RIM) * block_size, block_size)
            acc[target] += jnp.dot(
                weights[pair],
                edges[pl.ds(first, block_size)],
                preferred_element_type=jnp.float32,
            )

    @pl.loop(0, slots)
    def _(slot):
        stage[slot] = acc[slot].astype(jnp.bfloat16)
        block = slot_block[0, slot]

        @pl.when(block >= 0)
        def _():
            pltpu.make_async_copy(
                stage.at[slot], sums_out.at[block], store_sem.at[block]
            ).start()

    latent_copy.wait()

    @pl.loop(0, blocks)
    def _(block):
        pltpu.make_async_copy(zeros, sums_out.at[block], store_sem.at[block]).wait()


def ring_kernel(
    device_total,
    sums,
    aggregate,
    own,
    peer,
    got,
    own_sem,
    peer_send,
    peer_recv,
    ring_send,
    ring_recv,
):
    chips = device_total // 2
    per_owner = own.shape[1]
    width = own.shape[2]
    chains = per_owner // chain_rows
    me = lax.axis_index("blocks")
    chip = me // 2
    core = me % 2

    def chip_at(place):
        return jnp.where(place < chips // 2, 2 * place, 2 * (chips - 1 - place) + 1)

    place = jnp.where(chip % 2 == 0, chip // 2, chips - 1 - chip // 2)
    after = 2 * chip_at((place + 1) % chips) + core
    before = 2 * chip_at((place + chips - 1) % chips) + core
    other = 2 * chip + 1 - core

    barrier = pltpu.get_barrier_semaphore()
    for device in (other, after, before):
        pl.semaphore_signal(
            barrier, inc=1, device_id={"blocks": device}, device_id_type=pl.DeviceIdType.MESH
        )

    def owner_chip(step, way):
        if way == 0:
            return chip_at((place + 2 * chips - 1 - step) % chips)
        return chip_at((place + 1 + step) % chips)

    def rows_of(chain):
        return pl.ds(chain * chain_rows, chain_rows)

    def sums_rows(step, chain, which):
        way = 0 if chain < chains // 2 else 1
        first = (2 * owner_chip(step, way) + which) * per_owner + chain * chain_rows
        return sums.at[pl.ds(first, chain_rows)]

    def own_copy(step, chain):
        return pltpu.make_async_copy(
            sums_rows(step, chain, core),
            own.at[step, rows_of(chain)],
            own_sem.at[step, chain],
        )

    def peer_copy(step, chain):
        return pltpu.make_async_remote_copy(
            src_ref=sums_rows(step, chain, 1 - core),
            dst_ref=peer.at[step, rows_of(chain)],
            send_sem=peer_send.at[step, chain],
            recv_sem=peer_recv.at[step, chain],
            device_id={"blocks": other},
            device_id_type=pl.DeviceIdType.MESH,
        )

    def ring_copy(step, chain):
        return pltpu.make_async_remote_copy(
            src_ref=own.at[step, rows_of(chain)],
            dst_ref=got.at[step, rows_of(chain)],
            send_sem=ring_send.at[step, chain],
            recv_sem=ring_recv.at[step, chain],
            device_id={"blocks": after if chain < chains // 2 else before},
            device_id_type=pl.DeviceIdType.MESH,
        )

    ahead = 3
    order = [
        chain for pair in zip(range(chains // 2), range(chains // 2, chains)) for chain in pair
    ]

    @pl.loop(0, chips)
    def _(step):
        for chain in order:
            own_copy(step, chain).start()

    pl.semaphore_wait(barrier, 3)
    for step in range(ahead):
        for chain in order:
            peer_copy(step, chain).start()

    def both(step, chain):
        own_copy(step, chain).wait()
        peer_copy(step, chain).wait_recv()
        rows = rows_of(chain)
        return own[step, rows].astype(jnp.float32) + peer[step, rows].astype(jnp.float32)

    for chain in order:
        own[0, rows_of(chain)] = both(0, chain).astype(jnp.bfloat16)
        ring_copy(0, chain).start()

    @pl.loop(1, chips - 1)
    def _(step):
        @pl.when(step + ahead - 1 < chips)
        def _():
            for chain in order:
                peer_copy(step + ahead - 1, chain).start()

        for chain in order:
            held = both(step, chain)
            ring_copy(step - 1, chain).wait_recv()
            total = held + got[step - 1, rows_of(chain)].astype(jnp.float32)
            own[step, rows_of(chain)] = total.astype(jnp.bfloat16)
            ring_copy(step, chain).start()

    last = chips - 1
    for chain in order:
        held = both(last, chain)
        ring_copy(last - 1, chain).wait_recv()
        total = held + got[last - 1, rows_of(chain)].astype(jnp.float32)
        rows = rows_of(chain)
        aggregate[rows] = total.astype(jnp.bfloat16)

    @pl.loop(0, chips)
    def _(step):
        for chain in order:
            peer_copy(step, chain).wait_send()

    @pl.loop(0, chips - 1)
    def _(step):
        for chain in range(chains):
            ring_copy(step, chain).wait_send()


def mesh_kernel(
    aggregate, mesh_latent, w_mesh1, b_mesh1, w_mesh2, b_mesh2, mesh_gain, mesh_out, held, sem
):
    width = w_mesh2.shape[0]
    load = pltpu.make_async_copy(aggregate, held, sem)
    load.start()
    value = jnp.dot(mesh_latent[...], w_mesh1[:width], preferred_element_type=jnp.float32)
    load.wait()
    value += jnp.dot(held[...], w_mesh1[width:], preferred_element_type=jnp.float32)
    hidden = silu(value + b_mesh1[...]).astype(jnp.bfloat16)
    value = jnp.dot(hidden, w_mesh2[...], preferred_element_type=jnp.float32) + b_mesh2[...]
    update = layer_norm(value, mesh_gain[...])
    mesh_out[...] = (mesh_latent[...].astype(jnp.float32) + update).astype(jnp.bfloat16)


def on_device(
    features,
    pair_grid,
    pair_slot,
    slot_block,
    pair_count,
    coupling,
    mesh_latent,
    w_in,
    b_in,
    w_out,
    b_out,
    grid_gain,
    w_edge,
    w_mesh1,
    b_mesh1,
    w_mesh2,
    b_mesh2,
    mesh_gain,
):
    block_size = coupling.shape[-1]
    pair_total = coupling.shape[1]
    width = w_edge.shape[1]
    rows, feature_width = features.shape
    tile = RIM * block_size
    tiles = rows // tile
    owner_total = lax.axis_size("blocks")
    slot_total = slot_block.shape[1]
    features = features.T
    own_blocks = mesh_latent.shape[0] // block_size
    mesh_blocks = own_blocks * owner_total
    bf16 = jnp.bfloat16
    f32 = jnp.float32

    def flat(vector):
        return vector.reshape(1, -1)

    params = (w_in, flat(b_in), w_out, flat(b_out), flat(grid_gain), w_edge)
    param_specs = [pl.BlockSpec(param.shape, lambda i: (0, 0)) for param in params]
    wide = 2 * tile
    done_steps = rows // wide - 1
    smem = pl.BlockSpec(memory_space=pltpu.SMEM)
    anywhere = pl.BlockSpec(memory_space=pltpu.HBM)
    vmem = pl.BlockSpec(memory_space=pltpu.VMEM)
    semaphore = pltpu.SemaphoreType.DMA
    count = done_steps * wide

    left = lax.ppermute(
        features[:, rows - tile :],
        "blocks",
        [(i, (i + 1) % owner_total) for i in range(owner_total)],
    )
    right = lax.ppermute(
        features[:, :tile], "blocks", [((i + 1) % owner_total, i) for i in range(owner_total)]
    )

    latent, done = pl.pallas_call(
        grid_kernel,
        grid=(done_steps,),
        in_specs=[pl.BlockSpec((feature_width, wide), lambda i: (0, i))] + param_specs,
        out_specs=[
            pl.BlockSpec((wide, width), lambda i: (i, 0)),
            pl.BlockSpec((wide, width), lambda i: (i, 0)),
        ],
        out_shape=[
            jax.ShapeDtypeStruct((rows, width), bf16),
            jax.ShapeDtypeStruct((count, width), bf16),
        ],
        cost_estimate=pl.CostEstimate(
            flops=count * 2 * width * (feature_width + 2 * width),
            bytes_accessed=count * (feature_width + 2 * width) * 2,
            transcendentals=count * width,
        ),
        compiler_params=pltpu.CompilerParams(vmem_limit_bytes=grid_mib * mib),
        name="grid_rows",
    )(features, *params)

    pair_bytes = (rows + 2 * tile + 3 * slot_total * block_size) * width * 2
    pair_bytes += pair_total * block_size * block_size * 2
    grid_latent, sums = pl.pallas_call(
        pair_kernel,
        grid=(1,),
        in_specs=[smem] * 4
        + [pl.BlockSpec((feature_width, wide), lambda i: (0, done_steps))]
        + param_specs
        + [vmem, vmem, anywhere, anywhere, anywhere],
        out_specs=[anywhere, anywhere],
        out_shape=[
            jax.ShapeDtypeStruct((rows, width), bf16),
            jax.ShapeDtypeStruct((mesh_blocks, block_size, width), bf16),
        ],
        scratch_shapes=[
            pltpu.VMEM((rows + 2 * tile, width), bf16),
            pltpu.VMEM((pair_total, block_size, block_size), bf16),
            pltpu.VMEM((slot_total + 1, block_size, width), f32),
            pltpu.VMEM((slot_total, block_size, width), bf16),
            pltpu.VMEM((block_size, width), bf16),
            pltpu.VMEM((wide, width), bf16),
            semaphore((2,)),
            semaphore((mesh_blocks,)),
            semaphore,
        ],
        input_output_aliases={15: 0},
        compiler_params=pltpu.CompilerParams(vmem_limit_bytes=min(56 * mib, pair_bytes + spare_mib * mib)),
        name="pair_sums",
    )(
        pair_grid,
        pair_slot,
        slot_block,
        pair_count,
        features,
        *params,
        left,
        right,
        done,
        coupling,
        latent,
    )

    chips = owner_total // 2
    mesh_rows = own_blocks * block_size
    aggregate = pl.pallas_call(
        functools.partial(ring_kernel, owner_total),
        in_specs=[anywhere],
        out_specs=vmem,
        out_shape=jax.ShapeDtypeStruct(mesh_latent.shape, bf16),
        scratch_shapes=[
            pltpu.VMEM((chips, mesh_rows, width), bf16),
            pltpu.VMEM((chips, mesh_rows, width), bf16),
            pltpu.VMEM((chips - 1, mesh_rows, width), bf16),
            pltpu.SemaphoreType.DMA((chips, mesh_rows // chain_rows)),
            pltpu.SemaphoreType.DMA((chips, mesh_rows // chain_rows)),
            pltpu.SemaphoreType.DMA((chips, mesh_rows // chain_rows)),
            pltpu.SemaphoreType.DMA((chips - 1, mesh_rows // chain_rows)),
            pltpu.SemaphoreType.DMA((chips - 1, mesh_rows // chain_rows)),
        ],
        compiler_params=pltpu.CompilerParams(
            collective_id=0, has_side_effects=True, vmem_limit_bytes=56 * mib
        ),
        name="ring_sums",
    )(sums.reshape(-1, width))
    mesh_out = pl.pallas_call(
        mesh_kernel,
        in_specs=[anywhere] + [vmem] * 6,
        out_specs=vmem,
        out_shape=jax.ShapeDtypeStruct(mesh_latent.shape, bf16),
        scratch_shapes=[pltpu.VMEM(mesh_latent.shape, bf16), semaphore],
        compiler_params=pltpu.CompilerParams(vmem_limit_bytes=16 * mib),
        name="mesh_rows",
    )(aggregate, mesh_latent, w_mesh1, flat(b_mesh1), w_mesh2, flat(b_mesh2), flat(mesh_gain))
    return (grid_latent, mesh_out)


def solution(mesh):
    in_specs = (
        P(("groups", "blocks"), None),
        P("blocks", None),
        P("blocks", None),
        P("blocks", None),
        P("blocks"),
        P("blocks", None, None, None),
        P("blocks", None),
        P(),
        P(),
        P(),
        P(),
        P(),
        P(),
        P(),
        P(),
        P(),
        P(),
        P(),
    )
    out_specs = (P(("groups", "blocks"), None), P(("groups", "blocks"), None))
    return jax.shard_map(
        on_device, mesh=mesh, in_specs=in_specs, out_specs=out_specs, check_vma=False
    )
```
